256 devices in a mesh: orb: 4 (over y), grid: 64 (over z, x, core).
Axes of the slice: x: 4, y: 4, z: 8, core: 2. Of those that a mesh axis runs over, the one named last changes fastest.
Arguments:
- orbitals: float32 [4, 768, 192, 256], P('orb', 'grid'), may hold values from -6 to 6
- potential: float32 [768, 192, 256], P('grid'), may hold values from -4 to 0
- trial_potential: float32 [768, 192, 256], P('grid'), may hold values from -6 to 6
- eigenvalues: float32 [4], P('orb'), may hold values from -3 to 0
- frequency: float32 [1], replicated, may hold values from 1 to 8
Outputs:
- solutions: float32 [4, 768, 192, 256], P('orb', 'grid')
- density: float32 [768, 192, 256], P('grid', 'orb')
The draws below stay inside these ranges and needn't reach their ends.
All inputs are finite; a program needn't handle non-finite values.
Results may differ from the reference program's by a relative error of at most 0.0001.
Values sent between devices are 32-bit elements; how exact they have to be, the bound alone decides.
No kernel may reach another device: no remote copies, remote signals or barrier semaphores. Data moves between devices by JAX's collectives and lax.ppermute only.
A program may use at most 192 MiB of HBM per device.

```python
import math
import jax
import jax.numpy as jnp
from jax import lax

NY = 192
NZ = 256
ITERS = 2
NORB = 4
NX = 768


def level_of(stream_key, dims, cuts, low, top_value):
    factor_of = 1.0
    for position, blocks in cuts:
        heights = jax.random.uniform(jax.random.fold_in(jax.random.fold_in(stream_key, 6), position), (blocks,), jnp.float32, low / len(cuts), top_value / len(cuts))
        factor_of = factor_of * jnp.repeat(jnp.exp(heights), dims[position] // blocks).reshape((-1,) + (1,) * (len(dims) - 1 - position))
    return factor_of


def gaussian(own_key, shape, scale, most, split=(), kind=jnp.bfloat16):
    array = jax.random.normal(own_key, shape, jnp.float32) * scale
    if len(split) > 0:
        array = level_of(own_key, shape, split, -0.22, 0.18) * array
    return jnp.clip(array, min=-most, max=most).astype(kind)


def setup_inputs(seed: int = 0) -> dict:
    key_list = jax.random.split(jax.random.key(seed), 6)
    return {
        "orbitals": gaussian(key_list[0], (NORB, NX, NY, NZ), 1.0, 6.0, ((0, 4), (1, 64)), jnp.float32),
        "potential": jnp.clip(-4.0 + 4.0 * jax.random.uniform(key_list[1], (NX, NY, NZ), jnp.float32) ** level_of(key_list[1], (NX, NY, NZ), ((0, 64),), -0.2, 0.2), -4.0, 0.0),
        "trial_potential": gaussian(key_list[2], (NX, NY, NZ), 1.0, 6.0, ((0, 64),), jnp.float32),
        "eigenvalues": jnp.clip(-3.0 + 3.0 * jax.random.uniform(key_list[3], (NORB,), jnp.float32) ** level_of(key_list[3], (NORB,), ((0, 4),), -0.2, 0.2), -3.0, 0.0),
        "frequency": jnp.clip(jnp.exp(jax.random.uniform(key_list[4], (1,), jnp.float32, math.log(1.0), math.log(8.0))), 1.0, 8.0),
    }


STENCIL = (-5369.0 / 1800.0, 12.0 / 7.0, -15.0 / 56.0, 10.0 / 189.0, -1.0 / 112.0, 2.0 / 1925.0, -1.0 / 16632.0)
SPACING = 0.75


def shifted_hamiltonian(padded, potential, energy):
    axis_rows = padded.ndim - 3
    axis_cols = padded.ndim - 2
    length = padded.shape[axis_rows] - 12
    width = padded.shape[axis_cols]
    wrapped = jnp.concatenate([padded[..., width - 6:, :], padded, padded[..., :6, :]], axis=axis_cols)

    def take(row_off, col_off):
        part = lax.slice_in_dim(wrapped, 6 + row_off, 6 + row_off + length, axis=axis_rows)
        return lax.slice_in_dim(part, 6 + col_off, 6 + col_off + width, axis=axis_cols)

    center = take(0, 0)
    summed = 3.0 * STENCIL[0] * center
    for offset in range(1, 7):
        beside_all = take(offset, 0) + take(-offset, 0) + take(0, offset) + take(0, -offset)
        beside_all = beside_all + jnp.roll(center, offset, -1) + jnp.roll(center, -offset, -1)
        summed = summed + STENCIL[offset] * beside_all
    return (-0.5 / (SPACING * SPACING)) * summed + (potential - energy) * center


def pad_rows(field):
    return jnp.pad(field, ((6, 6), (0, 0), (0, 0)))


def reference(orbitals, potential, trial_potential, eigenvalues, frequency):
    squared = frequency[0] * frequency[0]

    def solve_one(item):
        orbital, energy = item

        def shifted(field):
            return shifted_hamiltonian(pad_rows(field), potential, energy)

        def operator(field):
            return shifted(shifted(field)) + squared * field

        source = trial_potential * orbital
        solution = jnp.zeros_like(source)
        residual = source
        direction = source
        norm_now = jnp.sum(residual * residual)
        for step in range(ITERS):
            image = operator(direction)
            step_size = norm_now / jnp.sum(direction * image)
            solution = solution + step_size * direction
            residual = residual - step_size * image
            norm_next = jnp.sum(residual * residual)
            direction = residual + (norm_next / norm_now) * direction
            norm_now = norm_next
        response = -4.0 * orbital * shifted(solution)
        return solution, response

    solutions, responses = lax.map(solve_one, (orbitals, eigenvalues))
    return solutions, jnp.sum(responses, axis=0)
```

```python
import functools

import jax
import jax.numpy as jnp
import ml_dtypes
import numpy as np
from jax import lax
from jax.experimental import pallas as pl
from jax.experimental.pallas import tpu as pltpu
from jax.sharding import PartitionSpec as P

STENCIL = (
    -5369.0 / 1800.0,
    12.0 / 7.0,
    -15.0 / 56.0,
    10.0 / 189.0,
    -1.0 / 112.0,
    2.0 / 1925.0,
    -1.0 / 16632.0,
)
SPACING = 0.75
COEF = tuple(-0.5 / (SPACING * SPACING) * c for c in STENCIL)
W = 6
F32, BF16 = jnp.float32, jnp.bfloat16
VM = pl.BlockSpec(memory_space=pltpu.VMEM)
SM = pl.BlockSpec(memory_space=pltpu.SMEM)
ANY = pl.BlockSpec(memory_space=pl.ANY)
MIB = 1 << 20


def in_hbm_type(array):
    return pltpu.HBM(array.shape, array.dtype)


def in_vmem(value):
    return pltpu.with_memory_space_constraint(value, pltpu.VMEM)


def in_hbm(value):
    return pltpu.with_memory_space_constraint(value, pltpu.HBM)


def circulant(n):
    m = np.zeros((n, n), np.float64)
    for k in range(1, W + 1):
        for i in range(n):
            m[i, (i + k) % n] += COEF[k]
            m[i, (i - k) % n] += COEF[k]
    high = m.astype(ml_dtypes.bfloat16)
    low = (m - high.astype(np.float64)).astype(ml_dtypes.bfloat16)
    return high, low


def plane_of(m, core):
    return m + core * (2 * W - 1 - 2 * m)


def core_index():
    return lax.rem(lax.axis_index("grid"), 2)


def rows_of(t):
    return pl.ds(pl.multiple_of(t * 8, 8), 8)


def call(kernel, out_shape, in_specs, out_specs, scratch=(), limit=24):
    return pl.pallas_call(
        kernel,
        out_shape=out_shape,
        in_specs=in_specs,
        out_specs=out_specs,
        scratch_shapes=list(scratch),
        compiler_params=pltpu.CompilerParams(vmem_limit_bytes=limit * MIB),
    )


def source_kernel(orb, trial, core_ref, ro, ri, a, b, sems):
    core = core_ref[0]

    def copies(m):
        p = plane_of(m, core)
        return (
            pltpu.make_async_copy(orb.at[0, p], a.at[m], sems.at[0, m]),
            pltpu.make_async_copy(trial.at[p], b.at[m], sems.at[1, m]),
        )

    for m in range(2 * W):
        for c in copies(m):
            c.start()
    for m in range(2 * W):
        for c in copies(m):
            c.wait()
        out = ro if m < W else ri
        out[m % W] = a[m] * b[m]


def part_rows(d, me, count, part):
    quarter = lax.rem(me + d, count)
    return quarter * part


def local_kernel(fo, fi, hi_halo, pot, orb, energy, core_ref, me_ref, mz, my, *refs, stage, count):
    gi, po, tile, own_out, kept, *parts = refs[-count - 9 : -5]
    orb_v, own, yz, sems, more_sems = refs[-5:]
    parts = [own, *parts]
    core, me = core_ref[0], me_ref[0]
    nz = fo.shape[2]
    part = own.shape[1]
    first = 0 if stage == 1 else W
    loads = [pltpu.make_async_copy(orb.at[0, plane_of(first + m, core)], orb_v.at[m], sems.at[m]) for m in range(W)]
    stores = (
        pltpu.make_async_copy(fo, kept.at[pl.ds(0, W)], more_sems.at[0]),
        pltpu.make_async_copy(fi, kept.at[pl.ds(W, W)], more_sems.at[1]),
    )
    store_own = pltpu.make_async_copy(own, own_out, more_sems.at[2])
    for c in loads:
        c.start()

    for half, ref in enumerate((fo, fi)):

        def one(m, _, ref=ref, half=half):
            v = ref[m]
            high = v.astype(BF16)
            low = (v - high.astype(F32)).astype(BF16)
            dot = functools.partial(jnp.dot, preferred_element_type=F32)
            acc = dot(high, mz[0]) + dot(low, mz[0]) + dot(high, mz[1])
            acc = acc + (dot(my[0], high) + dot(my[1], high) + dot(my[0], low))
            yz[half * W + m] = acc
            return 0

        lax.fori_loop(0, W, one, 0)

    for c in loads:
        c.wait()
    for c in stores:
        c.start()
    diag = 3.0 * COEF[0] - energy[0]
    acc = jnp.zeros((8, 128), F32)
    for d in range(count):
        start = part_rows(d, me, count, part)

        def column(t, acc, d=d, start=start):
            rows = pl.ds(pl.multiple_of(start + t * 8, 8), 8)
            for h in range(nz // 128):
                lanes = slice(128 * h, 128 * h + 128)
                line = [fo[m, rows, lanes] for m in range(W)]
                line += [fi[m, rows, lanes] for m in range(W)]
                line += [hi_halo[W - 1 - m, rows, lanes] for m in range(W)]
                for m in range(2 * W):
                    if stage < 2:
                        acc = acc + line[m] * line[m]
                    out = (pot[plane_of(m, core), rows, lanes] + diag) * line[m]
                    out = out + yz[m, rows, lanes]
                    for k in range(1, W + 1):
                        pair = line[m + k] if m < k else line[m + k] + line[m - k]
                        out = out + COEF[k] * pair
                    if m < W:
                        po[m, rows, lanes] = out
                        if stage == 1:
                            parts[d][m, rows_of(t), lanes] = orb_v[m, rows, lanes] * line[m]
                    else:
                        gi[m - W, rows, lanes] = out
                        if stage != 1:
                            at = m if stage == 2 and d else m - W
                            parts[d][at, rows_of(t), lanes] = orb_v[m - W, rows, lanes] * out
            return acc

        acc = lax.fori_loop(0, part // 8, column, acc)
    tile[...] = acc
    store_own.start()
    for c in stores:
        c.wait()
    store_own.wait()


def with_halo(po, ho, rows, lanes):
    halo = [ho[j, rows, lanes] for j in range(W)]
    outs = []
    for m in range(W):
        out = po[m, rows, lanes]
        for k in range(m + 1, W + 1):
            out = out + COEF[k] * halo[k - m - 1]
        outs.append(out)
    return outs


def halo_kernel(po, ho, *refs):
    go = refs[-1]

    def column(t, _):
        rows = rows_of(t)
        for h in range(po.shape[2] // 128):
            lanes = slice(128 * h, 128 * h + 128)
            for m, out in enumerate(with_halo(po, ho, rows, lanes)):
                go[m, rows, lanes] = out
        return 0

    lax.fori_loop(0, po.shape[1] // 8, column, 0)


def whole_sum(tile):
    return jnp.sum(tile, keepdims=True)


def broad(scalar, shape=(8, 128)):
    return jnp.broadcast_to(scalar, shape)


def sums_kernel(r, t_kept, orb, uo, ui, vi, rr_tile, tt_tile, core_ref, *refs):
    rows_out, inner, to, orb_o, r_v, ti, sems = refs[-7:]
    core = core_ref[0]
    ro, ri = r_v.at[pl.ds(0, W)], r_v.at[pl.ds(W, W)]
    loads = (
        pltpu.make_async_copy(r, r_v, sems.at[0]),
        pltpu.make_async_copy(t_kept.at[pl.ds(W, W)], ti, sems.at[1]),
        pltpu.make_async_copy(t_kept.at[pl.ds(0, W)], to, sems.at[2]),
        *(pltpu.make_async_copy(orb.at[0, plane_of(m, core)], orb_o.at[m], sems.at[3 + m]) for m in range(W)),
    )
    for c in loads:
        c.start()
    loads[0].wait()
    steps = uo.shape[1] // 8
    zero = jnp.zeros((8, 128), F32)

    def cells(t):
        for h in range(uo.shape[2] // 128):
            for m in range(W):
                yield m, rows_of(t), slice(128 * h, 128 * h + 128)

    def cross(t, acc):
        for at in cells(t):
            acc = acc + ro[at] * uo[at] + ri[at] * ui[at]
        return acc

    rr = whole_sum(rr_tile[...])
    ru = whole_sum(lax.fori_loop(0, steps, cross, zero))
    theta = broad(jnp.where(rr > 0.0, ru / jnp.where(rr > 0.0, rr, 1.0), 0.0))

    def squares(t, accs):
        s0, s1, t0, t1 = accs
        for at in cells(t):
            for r, u in ((ro, uo), (ri, ui)):
                x = u[at] - theta * r[at]
                s0, s1 = s0 + x * x, s1 + x * r[at]
            x = vi[at] - theta * ti[at]
            t0, t1 = t0 + x * x, t1 + x * ti[at]
        return s0, s1, t0, t1

    loads[1].wait()
    s0, s1, t0, t1 = lax.fori_loop(0, steps, squares, (zero,) * 4)
    row = [rr, whole_sum(tt_tile[...]), whole_sum(s0), whole_sum(s1)]
    rows_out[...] = jnp.concatenate([broad(x, (1, 128)) for x in row] + [theta[:4]], axis=0)
    inner[0], inner[1] = t0, t1
    for c in loads[2:]:
        c.wait()


def last_kernel(po, ho, to, orb, rows_in, inner, me_ref, *refs, count):
    tile, own_out, *outs, own, sem = refs[-count - 3 :]
    for done, out in zip(refs[: count - 1], outs):
        for m in range(W, 2 * W):
            out[m] = done[m]
    outs = [own, *outs]
    me = me_ref[0]
    theta = broad(rows_in[4:5])
    part = outs[0].shape[1]
    accs = inner[0], inner[1]
    for d in range(count):
        start = part_rows(d, me, count, part)

        def column(step, accs, d=d, start=start):
            t0, t1 = accs
            there = pl.ds(pl.multiple_of(start + step * 8, 8), 8)
            for h in range(po.shape[2] // 128):
                lanes = slice(128 * h, 128 * h + 128)
                for m, v in enumerate(with_halo(po, ho, there, lanes)):
                    t = to[m, there, lanes]
                    x = v - theta * t
                    t0, t1 = t0 + x * x, t1 + x * t
                    outs[d][m, rows_of(step), lanes] = orb[m, there, lanes] * v
            return t0, t1

        accs = lax.fori_loop(0, part // 8, column, accs)
        if d == 0:
            store_own = pltpu.make_async_copy(own, own_out, sem.at[0])
            store_own.start()
    lane = lax.broadcasted_iota(jnp.int32, (8, 128), 1)
    row = jnp.zeros((8, 128), F32)
    for i in range(5):
        row = jnp.where(lane == i, broad(rows_in[i : i + 1]), row)
    for i, x in enumerate(accs):
        row = jnp.where(lane == 5 + i, broad(whole_sum(x)), row)
    for i in range(tile.shape[0]):
        tile[i] = row
    store_own.wait()


def coefficient_kernel(shares, freq, out):
    w2 = freq[0] * freq[0]
    share = shares[:, 0, :]
    rr, tt, s0, s1, own, t0, t1 = (share[:, i : i + 1] for i in range(7))

    def total(x):
        return jnp.sum(x, axis=0, keepdims=True)

    rr0, tt0 = total(rr), total(tt)
    theta = tt0 / rr0
    off = jnp.broadcast_to(theta, own.shape) - own
    alpha = 1.0 / (theta + w2)
    rr1 = alpha * alpha * total(s0 - 2.0 * off * s1 + off * off * rr)
    tt1 = alpha * alpha * total(t0 - 2.0 * off * t1 + off * off * tt)
    ratio = rr1 / rr0
    beta = rr1 / (tt1 + w2 * rr1 - ratio * rr1 / alpha)
    p = alpha + beta * ratio + beta * alpha * theta
    q = -beta * alpha
    both = jnp.concatenate([broad(p, (4, 128)), broad(q, (4, 128))], axis=0)
    for i in range(out.shape[0]):
        out[i] = both


def both_of(coefs, n, shape):
    one = coefs[n]
    return tuple(broad(one[4 * i : 4 * i + 1, 0:1], shape) for i in range(2))


def solution_kernel(r, u, coefs, core_ref, sol, rbuf, ubuf, xbuf, in_sems, out_sems):
    core = core_ref[0]

    def fields(m):
        return (
            pltpu.make_async_copy(r.at[m], rbuf.at[m], in_sems.at[0, m]),
            pltpu.make_async_copy(u.at[m], ubuf.at[m], in_sems.at[1, m]),
        )

    def store(m):
        return pltpu.make_async_copy(xbuf.at[m], sol.at[0, plane_of(m, core)], out_sems.at[m])

    for m in range(2 * W):
        for c in fields(m):
            c.start()
    p, q = both_of(coefs, 0, (8, rbuf.shape[2]))
    for m in range(2 * W):
        for c in fields(m):
            c.wait()

        def row(t, _, m=m):
            rows = rows_of(t)
            xbuf[m, rows, :] = p * rbuf[m, rows, :] + q * ubuf[m, rows, :]
            return 0

        lax.fori_loop(0, rbuf.shape[1] // 8, row, 0, unroll=8)
        store(m).start()
    for m in range(2 * W):
        store(m).wait()


def density_kernel(coefs, core_ref, me_ref, *refs, count):
    ti, to, own_v, parts = refs[:count], refs[count : 2 * count], refs[2 * count : 2 * count + 2], refs[2 * count + 2 : -6]
    dens, t_all, own, dbuf, load_sems, sems = refs[-6:]
    parts = [own, *parts]
    core, me = core_ref[0], me_ref[0]
    loads = [[], []]
    for half, sources in enumerate((to, ti)):
        places = pl.ds(half * W, W)
        pairs = [(x, t_all.at[d, places]) for d, x in enumerate(sources)] + [(own_v[half], own.at[places])]
        loads[half] = [pltpu.make_async_copy(x, y, load_sems.at[half, i]) for i, (x, y) in enumerate(pairs)]
    for c in loads[0] + loads[1]:
        c.start()
    pq = [both_of(coefs, lax.rem(me - d + count, count), (8, own.shape[2])) for d in range(count)]
    pq = [(-4.0 * p, -4.0 * q) for p, q in pq]

    def store(m):
        return pltpu.make_async_copy(dbuf.at[m], dens.at[plane_of(m, core)], sems.at[m])

    for m in range(2 * W):
        if m % W == 0:
            for c in loads[m // W]:
                c.wait()

        def part(t, _, m=m):
            rows = rows_of(t)
            acc = None
            for d in range(count):
                term = pq[d][0] * t_all[d, m, rows, :] + pq[d][1] * parts[d][m, rows, :]
                acc = term if acc is None else acc + term
            dbuf[m, rows, :] = acc
            return 0

        lax.fori_loop(0, dbuf.shape[1] // 8, part, 0, unroll=2)
        store(m).start()
    for m in range(2 * W):
        store(m).wait()


def shift(value, axis, count, d):
    return lax.ppermute(value, axis, [(i, (i + d) % count) for i in range(count)])


def body(orbitals, potential, trial_potential, eigenvalues, frequency, *, norb, ngrid):
    _, nx, ny, nz = orbitals.shape
    half = pltpu.VMEM((W, ny, nz), F32)
    tile = jax.ShapeDtypeStruct((8, 128), F32)
    part = ny // norb
    whole = jax.ShapeDtypeStruct((2 * W, ny, nz), F32)
    piece = pltpu.VMEM((W, part, nz), F32)
    long_piece = pltpu.VMEM((2 * W, part, nz), F32)
    core = core_index().astype(jnp.int32).reshape(1)
    me = lax.axis_index("orb").astype(jnp.int32).reshape(1)
    mz = jnp.asarray(np.stack(circulant(nz)))
    my = jnp.asarray(np.stack(circulant(ny)))
    orbitals, trial_potential = in_hbm(orbitals), in_hbm(trial_potential)

    inner_pairs = [(i, i ^ 1) for i in range(ngrid)]
    outer_pairs = [(i, i + 1) for i in range(1, ngrid - 1, 2)]
    outer_pairs += [(j, i) for i, j in outer_pairs]

    def outer_swap(x):
        with jax.named_scope("outer_swap"):
            return in_vmem(lax.ppermute(x, "grid", outer_pairs))

    def inner_swap(x):
        with jax.named_scope("inner_swap"):
            return in_vmem(lax.ppermute(x, "grid", inner_pairs))

    def local(stage, fo, fi, hi, *after):
        parts_type = long_piece if stage == 2 else piece
        gi, po, out, own, kept, *parts = call(
            functools.partial(local_kernel, stage=stage, count=norb),
            (half, half, tile, in_hbm_type(piece), in_hbm_type(whole)) + (parts_type,) * (norb - 1),
            [VM] * 4 + [ANY, SM, SM, SM, VM, VM] + [ANY] * len(after),
            (VM, VM, VM, ANY, ANY) + (VM,) * (norb - 1),
            [
                pltpu.VMEM(half.shape, F32),
                pltpu.VMEM(piece.shape, F32),
                pltpu.VMEM(whole.shape, F32),
                pltpu.SemaphoreType.DMA((W,)),
                pltpu.SemaphoreType.DMA((3,)),
            ],
            limit=10,
        )(fo, fi, hi, potential, orbitals, eigenvalues, core, me, mz, my, *after)
        return gi, po, out, kept, [own, *parts]

    def add_halo(po, ho, *after):
        return call(halo_kernel, half, [VM, VM] + [VM] * len(after), VM, limit=4)(po, ho, *after)

    def send_parts(parts):
        with jax.named_scope("density_parts"):
            return [parts[0]] + [shift(parts[d], "orb", norb, d) for d in range(1, norb)]

    ro, ri = call(
        source_kernel,
        (half, half),
        [ANY, ANY, SM],
        (VM, VM),
        [pltpu.VMEM(whole.shape, F32), pltpu.VMEM(whole.shape, F32), pltpu.SemaphoreType.DMA((2, 2 * W))],
        limit=10,
    )(orbitals, trial_potential, core)
    ho = outer_swap(ro)
    ti, po, rr, r_kept, parts = local(0, ro, ri, inner_swap(ri))
    parts_ti = send_parts(parts)
    to = add_halo(po, ho)

    ho = outer_swap(to)
    ui, po, tt, t_kept, parts = local(1, to, ti, inner_swap(ti))
    parts_to = send_parts(parts)
    uo = add_halo(po, ho, *parts_ti[1:])

    ho = outer_swap(uo)
    vi, po, _, u_kept, parts = local(2, uo, ui, inner_swap(ui))
    shares, inner, to, orb_o = call(
        sums_kernel,
        (tile, jax.ShapeDtypeStruct((2, 8, 128), F32), half, half),
        [ANY] * 3 + [VM] * 5 + [SM],
        (VM,) * 4,
        [pltpu.VMEM(whole.shape, F32), pltpu.VMEM(half.shape, F32), pltpu.SemaphoreType.DMA((3 + W,))],
        limit=5,
    )(r_kept, t_kept, orbitals, uo, ui, vi, rr, tt, core)

    shares, own_vo, *parts_v = call(
        functools.partial(last_kernel, count=norb),
        (jax.ShapeDtypeStruct((ngrid, 8, 128), F32), in_hbm_type(piece)) + (long_piece,) * (norb - 1),
        [VM] * 6 + [SM] + [VM] * (2 * norb - 2),
        (VM, ANY) + (VM,) * (norb - 1),
        [pltpu.VMEM(piece.shape, F32), pltpu.SemaphoreType.DMA((1,))],
        limit=8,
    )(po, ho, to, orb_o, shares, inner, me, *parts[1:], *parts_to[1:])
    with jax.named_scope("density_parts"):
        parts_v = [in_vmem(shift(x, "orb", norb, d)) for d, x in enumerate(parts_v, 1)]
    with jax.named_scope("all_shares"):
        shares = lax.all_to_all(shares, "grid", 0, 0, tiled=True)
    coefs = call(coefficient_kernel, jax.ShapeDtypeStruct((norb, 8, 128), F32), [VM, SM], VM, limit=2)(
        shares, frequency
    )
    with jax.named_scope("all_coefficients"):
        all_coefs = lax.all_to_all(coefs, "orb", 0, 0, tiled=True)
    solution = call(
        solution_kernel,
        in_hbm_type(jax.ShapeDtypeStruct((1, nx, ny, nz), F32)),
        [ANY, ANY, VM, SM],
        ANY,
        [pltpu.VMEM(whole.shape, F32)] * 3 + [pltpu.SemaphoreType.DMA((2, nx)), pltpu.SemaphoreType.DMA((nx,))],
        limit=9,
    )(in_hbm(r_kept), in_hbm(u_kept), coefs, core)
    waiting = [in_hbm(x) for x in (*parts_ti, *parts_to, own_vo, parts[0])]
    density = call(
        functools.partial(density_kernel, count=norb),
        in_hbm_type(long_piece),
        [VM, SM, SM] + [ANY] * len(waiting) + [VM] * (norb - 1),
        ANY,
        [
            pltpu.VMEM((norb, *long_piece.shape), F32),
            pltpu.VMEM(long_piece.shape, F32),
            pltpu.VMEM(long_piece.shape, F32),
            pltpu.SemaphoreType.DMA((2, norb + 1)),
            pltpu.SemaphoreType.DMA((nx,)),
        ],
        limit=8,
    )(all_coefs, core, me, *waiting, *parts_v)
    return solution, density


def solution(mesh):
    in_specs = (
        P("orb", "grid", None, None),
        P("grid", None, None),
        P("grid", None, None),
        P("orb"),
        P(),
    )
    out_specs = (P("orb", "grid", None, None), P("grid", "orb", None))
    step = functools.partial(body, norb=mesh.shape["orb"], ngrid=mesh.shape["grid"])
    return jax.shard_map(step, mesh=mesh, in_specs=in_specs, out_specs=out_specs, check_vma=False)
```

```python
import functools

import jax
import jax.numpy as jnp
import ml_dtypes
import numpy as np
from jax import lax
from jax.experimental import pallas as pl
from jax.experimental.pallas import tpu as pltpu
from jax.sharding import PartitionSpec as P

STENCIL = (
    -5369.0 / 1800.0,
    12.0 / 7.0,
    -15.0 / 56.0,
    10.0 / 189.0,
    -1.0 / 112.0,
    2.0 / 1925.0,
    -1.0 / 16632.0,
)
SPACING = 0.75
COEF = tuple(-0.5 / (SPACING * SPACING) * c for c in STENCIL)
W = 6
F32, BF16 = jnp.float32, jnp.bfloat16
VM = pl.BlockSpec(memory_space=pltpu.VMEM)
SM = pl.BlockSpec(memory_space=pltpu.SMEM)
ANY = pl.BlockSpec(memory_space=pl.ANY)
MIB = 1 << 20
GRID = ("chip", "core")


def in_hbm_type(array):
    return pltpu.HBM(array.shape, array.dtype)


def in_vmem(value):
    return pltpu.with_memory_space_constraint(value, pltpu.VMEM)


def in_hbm(value):
    return pltpu.with_memory_space_constraint(value, pltpu.HBM)


def circulant(n):
    m = np.zeros((n, n), np.float64)
    for k in range(1, W + 1):
        for i in range(n):
            m[i, (i + k) % n] += COEF[k]
            m[i, (i - k) % n] += COEF[k]
    high = m.astype(ml_dtypes.bfloat16)
    low = (m - high.astype(np.float64)).astype(ml_dtypes.bfloat16)
    return high, low


def plane_of(m, core):
    return m + core * (2 * W - 1 - 2 * m)


def core_index():
    return lax.axis_index("core")


def rows_of(t):
    return pl.ds(pl.multiple_of(t * 8, 8), 8)


def call(kernel, out_shape, in_specs, out_specs, scratch=(), limit=24):
    return pl.pallas_call(
        kernel,
        out_shape=out_shape,
        in_specs=in_specs,
        out_specs=out_specs,
        scratch_shapes=list(scratch),
        compiler_params=pltpu.CompilerParams(vmem_limit_bytes=limit * MIB),
    )


def source_kernel(orb, trial, ro, ri, a, b, sems):
    core = core_index()

    def copies(m):
        p = plane_of(m, core)
        return (
            pltpu.make_async_copy(orb.at[0, p], a.at[m], sems.at[0, m]),
            pltpu.make_async_copy(trial.at[p], b.at[m], sems.at[1, m]),
        )

    for m in range(2 * W):
        for c in copies(m):
            c.start()
    for m in range(2 * W):
        for c in copies(m):
            c.wait()
        out = ro if m < W else ri
        out[m % W] = a[m] * b[m]


def part_rows(d, me, count, part):
    quarter = lax.rem(me + d, count)
    return quarter * part


def local_kernel(fo, fi, hi_halo, pot, orb, energy, mz, my, *refs, stage, count):
    gi, po, tile, own_out, kept, *parts = refs[-count - 9 : -5]
    orb_v, own, yz, sems, more_sems = refs[-5:]
    parts = [own, *parts]
    core, me = core_index(), lax.axis_index("orb")
    nz = fo.shape[2]
    part = own.shape[1]
    first = 0 if stage == 1 else W
    loads = [pltpu.make_async_copy(orb.at[0, plane_of(first + m, core)], orb_v.at[m], sems.at[m]) for m in range(W)]
    stores = (
        pltpu.make_async_copy(fo, kept.at[pl.ds(0, W)], more_sems.at[0]),
        pltpu.make_async_copy(fi, kept.at[pl.ds(W, W)], more_sems.at[1]),
    )
    store_own = pltpu.make_async_copy(own, own_out, more_sems.at[2])
    for c in loads:
        c.start()

    for half, ref in enumerate((fo, fi)):

        def one(m, _, ref=ref, half=half):
            v = ref[m]
            high = v.astype(BF16)
            low = (v - high.astype(F32)).astype(BF16)
            dot = functools.partial(jnp.dot, preferred_element_type=F32)
            acc = dot(high, mz[0]) + dot(low, mz[0]) + dot(high, mz[1])
            acc = acc + (dot(my[0], high) + dot(my[1], high) + dot(my[0], low))
            yz[half * W + m] = acc
            return 0

        lax.fori_loop(0, W, one, 0)

    for c in loads:
        c.wait()
    for c in stores:
        c.start()
    diag = 3.0 * COEF[0] - energy[0]
    acc = jnp.zeros((8, 128), F32)
    for d in range(count):
        start = part_rows(d, me, count, part)

        def column(t, acc, d=d, start=start):
            rows = pl.ds(pl.multiple_of(start + t * 8, 8), 8)
            for h in range(nz // 128):
                lanes = slice(128 * h, 128 * h + 128)
                line = [fo[m, rows, lanes] for m in range(W)]
                line += [fi[m, rows, lanes] for m in range(W)]
                line += [hi_halo[W - 1 - m, rows, lanes] for m in range(W)]
                for m in range(2 * W):
                    if stage < 2:
                        acc = acc + line[m] * line[m]
                    out = (pot[plane_of(m, core), rows, lanes] + diag) * line[m]
                    out = out + yz[m, rows, lanes]
                    for k in range(1, W + 1):
                        pair = line[m + k] if m < k else line[m + k] + line[m - k]
                        out = out + COEF[k] * pair
                    if m < W:
                        po[m, rows, lanes] = out
                        if stage == 1:
                            parts[d][m, rows_of(t), lanes] = orb_v[m, rows, lanes] * line[m]
                    else:
                        gi[m - W, rows, lanes] = out
                        if stage != 1:
                            at = m if stage == 2 and d else m - W
                            parts[d][at, rows_of(t), lanes] = orb_v[m - W, rows, lanes] * out
            return acc

        acc = lax.fori_loop(0, part // 8, column, acc)
    tile[...] = acc
    store_own.start()
    for c in stores:
        c.wait()
    store_own.wait()


def with_halo(po, ho, rows, lanes):
    halo = [ho[j, rows, lanes] for j in range(W)]
    outs = []
    for m in range(W):
        out = po[m, rows, lanes]
        for k in range(m + 1, W + 1):
            out = out + COEF[k] * halo[k - m - 1]
        outs.append(out)
    return outs


def halo_kernel(po, ho, *refs):
    go = refs[-1]

    def column(t, _):
        rows = rows_of(t)
        for h in range(po.shape[2] // 128):
            lanes = slice(128 * h, 128 * h + 128)
            for m, out in enumerate(with_halo(po, ho, rows, lanes)):
                go[m, rows, lanes] = out
        return 0

    lax.fori_loop(0, po.shape[1] // 8, column, 0)


def whole_sum(tile):
    return jnp.sum(tile, keepdims=True)


def broad(scalar, shape=(8, 128)):
    return jnp.broadcast_to(scalar, shape)


def sums_kernel(r, t_kept, orb, uo, ui, vi, rr_tile, tt_tile, *refs):
    rows_out, inner, to, orb_o, r_v, ti, sems = refs[-7:]
    core = core_index()
    ro, ri = r_v.at[pl.ds(0, W)], r_v.at[pl.ds(W, W)]
    loads = (
        pltpu.make_async_copy(r, r_v, sems.at[0]),
        pltpu.make_async_copy(t_kept.at[pl.ds(W, W)], ti, sems.at[1]),
        pltpu.make_async_copy(t_kept.at[pl.ds(0, W)], to, sems.at[2]),
        *(pltpu.make_async_copy(orb.at[0, plane_of(m, core)], orb_o.at[m], sems.at[3 + m]) for m in range(W)),
    )
    for c in loads:
        c.start()
    loads[0].wait()
    steps = uo.shape[1] // 8
    zero = jnp.zeros((8, 128), F32)

    def cells(t):
        for h in range(uo.shape[2] // 128):
            for m in range(W):
                yield m, rows_of(t), slice(128 * h, 128 * h + 128)

    def cross(t, acc):
        for at in cells(t):
            acc = acc + ro[at] * uo[at] + ri[at] * ui[at]
        return acc

    rr = whole_sum(rr_tile[...])
    ru = whole_sum(lax.fori_loop(0, steps, cross, zero))
    theta = broad(jnp.where(rr > 0.0, ru / jnp.where(rr > 0.0, rr, 1.0), 0.0))

    def squares(t, accs):
        s0, s1, t0, t1 = accs
        for at in cells(t):
            for r, u in ((ro, uo), (ri, ui)):
                x = u[at] - theta * r[at]
                s0, s1 = s0 + x * x, s1 + x * r[at]
            x = vi[at] - theta * ti[at]
            t0, t1 = t0 + x * x, t1 + x * ti[at]
        return s0, s1, t0, t1

    loads[1].wait()
    s0, s1, t0, t1 = lax.fori_loop(0, steps, squares, (zero,) * 4)
    row = [rr, whole_sum(tt_tile[...]), whole_sum(s0), whole_sum(s1)]
    rows_out[...] = jnp.concatenate([broad(x, (1, 128)) for x in row] + [theta[:4]], axis=0)
    inner[0], inner[1] = t0, t1
    for c in loads[2:]:
        c.wait()


def last_kernel(po, ho, to, orb, rows_in, inner, *refs, count):
    tile, own_out, *outs, own, sem = refs[-count - 3 :]
    for done, out in zip(refs[: count - 1], outs):
        for m in range(W, 2 * W):
            out[m] = done[m]
    outs = [own, *outs]
    me = lax.axis_index("orb")
    theta = broad(rows_in[4:5])
    part = outs[0].shape[1]
    accs = inner[0], inner[1]
    for d in range(count):
        start = part_rows(d, me, count, part)

        def column(step, accs, d=d, start=start):
            t0, t1 = accs
            there = pl.ds(pl.multiple_of(start + step * 8, 8), 8)
            for h in range(po.shape[2] // 128):
                lanes = slice(128 * h, 128 * h + 128)
                for m, v in enumerate(with_halo(po, ho, there, lanes)):
                    t = to[m, there, lanes]
                    x = v - theta * t
                    t0, t1 = t0 + x * x, t1 + x * t
                    outs[d][m, rows_of(step), lanes] = orb[m, there, lanes] * v
            return t0, t1

        accs = lax.fori_loop(0, part // 8, column, accs)
        if d == 0:
            store_own = pltpu.make_async_copy(own, own_out, sem.at[0])
            store_own.start()
    lane = lax.broadcasted_iota(jnp.int32, (8, 128), 1)
    row = jnp.zeros((8, 128), F32)
    for i in range(5):
        row = jnp.where(lane == i, broad(rows_in[i : i + 1]), row)
    for i, x in enumerate(accs):
        row = jnp.where(lane == 5 + i, broad(whole_sum(x)), row)
    tile[...] = row
    store_own.wait()


def copies_kernel(row, other, out):
    mine = lax.broadcasted_iota(jnp.int32, row.shape, 0) == core_index()
    both = jnp.where(mine, row[...], other[...])
    for i in range(out.shape[0]):
        out[i] = both


def preload_kernel(field, out, sem):
    load = pltpu.make_async_copy(field, out, sem.at[0])
    load.start()
    load.wait()


def coefficient_kernel(shares, freq, *refs):
    out = refs[-1]
    w2 = freq[0] * freq[0]
    share = jnp.concatenate([shares[:, 0, :], shares[:, 1, :]], axis=0)
    rr, tt, s0, s1, own, t0, t1 = (share[:, i : i + 1] for i in range(7))

    def total(x):
        return jnp.sum(x, axis=0, keepdims=True)

    rr0, tt0 = total(rr), total(tt)
    theta = tt0 / rr0
    off = jnp.broadcast_to(theta, own.shape) - own
    alpha = 1.0 / (theta + w2)
    rr1 = alpha * alpha * total(s0 - 2.0 * off * s1 + off * off * rr)
    tt1 = alpha * alpha * total(t0 - 2.0 * off * t1 + off * off * tt)
    ratio = rr1 / rr0
    beta = rr1 / (tt1 + w2 * rr1 - ratio * rr1 / alpha)
    p = alpha + beta * ratio + beta * alpha * theta
    q = -beta * alpha
    both = jnp.concatenate([broad(p, (4, 128)), broad(q, (4, 128))], axis=0)
    for i in range(out.shape[0]):
        out[i] = both


def both_of(coefs, n, shape):
    one = coefs[n]
    return tuple(broad(one[4 * i : 4 * i + 1, 0:1], shape) for i in range(2))


def solution_kernel(r, u, coefs, sol, rbuf, xbuf, in_sems, out_sems):
    core = core_index()

    def field(m):
        return pltpu.make_async_copy(r.at[m], rbuf.at[m], in_sems.at[m])

    def store(m):
        return pltpu.make_async_copy(xbuf.at[m], sol.at[0, plane_of(m, core)], out_sems.at[m])

    for m in range(2 * W):
        field(m).start()
    p, q = both_of(coefs, 0, (8, r.shape[2]))
    for m in range(2 * W):
        field(m).wait()

        def row(t, _, m=m):
            rows = rows_of(t)
            xbuf[m, rows, :] = p * rbuf[m, rows, :] + q * u[m, rows, :]
            return 0

        lax.fori_loop(0, r.shape[1] // 8, row, 0, unroll=8)
        store(m).start()
    for m in range(2 * W):
        store(m).wait()


def density_kernel(coefs, *refs, count):
    ti, to, own_v, parts = refs[:count], refs[count : 2 * count], refs[2 * count : 2 * count + 2], refs[2 * count + 2 : -6]
    dens, t_all, own, dbuf, load_sems, sems = refs[-6:]
    parts = [own, *parts]
    core, me = core_index(), lax.axis_index("orb")
    loads = [[], []]
    for half, sources in enumerate((to, ti)):
        places = pl.ds(half * W, W)
        pairs = [(x, t_all.at[d, places]) for d, x in enumerate(sources)] + [(own_v[half], own.at[places])]
        loads[half] = [pltpu.make_async_copy(x, y, load_sems.at[half, i]) for i, (x, y) in enumerate(pairs)]
    for c in loads[0] + loads[1]:
        c.start()
    pq = [both_of(coefs, lax.rem(me - d + count, count), (8, own.shape[2])) for d in range(count)]
    pq = [(-4.0 * p, -4.0 * q) for p, q in pq]

    def store(m):
        return pltpu.make_async_copy(dbuf.at[m], dens.at[plane_of(m, core)], sems.at[m])

    for m in range(2 * W):
        if m % W == 0:
            for c in loads[m // W]:
                c.wait()

        def part(t, _, m=m):
            rows = rows_of(t)
            acc = None
            for d in range(count):
                term = pq[d][0] * t_all[d, m, rows, :] + pq[d][1] * parts[d][m, rows, :]
                acc = term if acc is None else acc + term
            dbuf[m, rows, :] = acc
            return 0

        lax.fori_loop(0, dbuf.shape[1] // 8, part, 0, unroll=2)
        store(m).start()
    for m in range(2 * W):
        store(m).wait()


def shift(value, axis, count, d):
    return lax.ppermute(value, axis, [(i, (i + d) % count) for i in range(count)])


def body(orbitals, potential, trial_potential, eigenvalues, frequency, *, norb, ngrid):
    _, nx, ny, nz = orbitals.shape
    half = pltpu.VMEM((W, ny, nz), F32)
    tile = jax.ShapeDtypeStruct((8, 128), F32)
    part = ny // norb
    whole = jax.ShapeDtypeStruct((2 * W, ny, nz), F32)
    piece = pltpu.VMEM((W, part, nz), F32)
    long_piece = pltpu.VMEM((2 * W, part, nz), F32)
    mz = jnp.asarray(np.stack(circulant(nz)))
    my = jnp.asarray(np.stack(circulant(ny)))
    orbitals, trial_potential = in_hbm(orbitals), in_hbm(trial_potential)

    inner_pairs = [(i, i ^ 1) for i in range(ngrid)]
    outer_pairs = [(i, i + 1) for i in range(1, ngrid - 1, 2)]
    outer_pairs += [(j, i) for i, j in outer_pairs]

    def outer_swap(x):
        with jax.named_scope("outer_swap"):
            return in_vmem(lax.ppermute(x, GRID, outer_pairs))

    def inner_swap(x):
        with jax.named_scope("inner_swap"):
            return in_vmem(lax.ppermute(x, GRID, inner_pairs))

    def local(stage, fo, fi, hi, *after):
        parts_type = long_piece if stage == 2 else piece
        gi, po, out, own, kept, *parts = call(
            functools.partial(local_kernel, stage=stage, count=norb),
            (half, half, tile, in_hbm_type(piece), in_hbm_type(whole)) + (parts_type,) * (norb - 1),
            [VM] * 4 + [ANY, SM, VM, VM] + [ANY] * len(after),
            (VM, VM, VM, ANY, ANY) + (VM,) * (norb - 1),
            [
                pltpu.VMEM(half.shape, F32),
                pltpu.VMEM(piece.shape, F32),
                pltpu.VMEM(whole.shape, F32),
                pltpu.SemaphoreType.DMA((W,)),
                pltpu.SemaphoreType.DMA((3,)),
            ],
            limit=12,
        )(fo, fi, hi, potential, orbitals, eigenvalues, mz, my, *after)
        return gi, po, out, kept, [own, *parts]

    def add_halo(po, ho, *after):
        return call(halo_kernel, half, [VM, VM] + [VM] * len(after), VM, limit=4)(po, ho, *after)

    def send_parts(parts):
        with jax.named_scope("density_parts"):
            return [parts[0]] + [shift(parts[d], "orb", norb, d) for d in range(1, norb)]

    ro, ri = call(
        source_kernel,
        (half, half),
        [ANY, ANY],
        (VM, VM),
        [pltpu.VMEM(whole.shape, F32), pltpu.VMEM(whole.shape, F32), pltpu.SemaphoreType.DMA((2, 2 * W))],
        limit=10,
    )(orbitals, trial_potential)
    ho = outer_swap(ro)
    ti, po, rr, r_kept, parts = local(0, ro, ri, inner_swap(ri))
    parts_ti = send_parts(parts)
    to = add_halo(po, ho)

    ho = outer_swap(to)
    ui, po, tt, t_kept, parts = local(1, to, ti, inner_swap(ti))
    parts_to = send_parts(parts)
    uo = add_halo(po, ho, *parts_ti[1:])

    ho = outer_swap(uo)
    vi, po, _, u_kept, parts = local(2, uo, ui, inner_swap(ui))
    shares, inner, to, orb_o = call(
        sums_kernel,
        (tile, jax.ShapeDtypeStruct((2, 8, 128), F32), half, half),
        [ANY] * 3 + [VM] * 5,
        (VM,) * 4,
        [pltpu.VMEM(whole.shape, F32), pltpu.VMEM(half.shape, F32), pltpu.SemaphoreType.DMA((3 + W,))],
        limit=5,
    )(r_kept, t_kept, orbitals, uo, ui, vi, rr, tt)

    shares, own_vo, *parts_v = call(
        functools.partial(last_kernel, count=norb),
        (tile, in_hbm_type(piece)) + (long_piece,) * (norb - 1),
        [VM] * (4 + 2 * norb),
        (VM, ANY) + (VM,) * (norb - 1),
        [pltpu.VMEM(piece.shape, F32), pltpu.SemaphoreType.DMA((1,))],
        limit=8,
    )(po, ho, to, orb_o, shares, inner, *parts[1:], *parts_to[1:])
    with jax.named_scope("density_parts"):
        parts_v = [in_vmem(shift(x, "orb", norb, d)) for d, x in enumerate(parts_v, 1)]
    with jax.named_scope("all_shares"):
        shares = call(
            copies_kernel, jax.ShapeDtypeStruct((ngrid // 2, 8, 128), F32), [VM, VM], VM, limit=4
        )(shares, lax.ppermute(shares, GRID, inner_pairs))
        shares = lax.all_to_all(shares, "chip", 0, 0, tiled=True)
    u_all = call(preload_kernel, whole, [ANY], VM, [pltpu.SemaphoreType.DMA((1,))], limit=4)(in_hbm(u_kept))
    coefs = call(coefficient_kernel, jax.ShapeDtypeStruct((norb, 8, 128), F32), [VM, SM, VM], VM, limit=4)(
        shares, frequency, u_all
    )
    with jax.named_scope("all_coefficients"):
        all_coefs = lax.all_to_all(coefs, "orb", 0, 0, tiled=True)
    solution = call(
        solution_kernel,
        in_hbm_type(jax.ShapeDtypeStruct((1, nx, ny, nz), F32)),
        [ANY, VM, VM],
        ANY,
        [pltpu.VMEM(whole.shape, F32)] * 2 + [pltpu.SemaphoreType.DMA((nx,))] * 2,
        limit=9,
    )(in_hbm(r_kept), u_all, coefs)
    waiting = [in_hbm(x) for x in (*parts_ti, *parts_to, own_vo, parts[0])]
    density = call(
        functools.partial(density_kernel, count=norb),
        in_hbm_type(long_piece),
        [VM] + [ANY] * len(waiting) + [VM] * (norb - 1),
        ANY,
        [
            pltpu.VMEM((norb, *long_piece.shape), F32),
            pltpu.VMEM(long_piece.shape, F32),
            pltpu.VMEM(long_piece.shape, F32),
            pltpu.SemaphoreType.DMA((2, norb + 1)),
            pltpu.SemaphoreType.DMA((nx,)),
        ],
        limit=8,
    )(all_coefs, *waiting, *parts_v)
    return solution, density


def solution(mesh):
    norb, ngrid = mesh.shape["orb"], mesh.shape["grid"]
    mesh = jax.sharding.Mesh(mesh.devices.reshape(norb, ngrid // 2, 2), ("orb", *GRID))
    in_specs = (
        P("orb", GRID, None, None),
        P(GRID, None, None),
        P(GRID, None, None),
        P("orb"),
        P(),
    )
    out_specs = (P("orb", GRID, None, None), P(GRID, "orb", None))
    step = functools.partial(body, norb=norb, ngrid=ngrid)
    return jax.shard_map(step, mesh=mesh, in_specs=in_specs, out_specs=out_specs, check_vma=False)
```

```python
import functools

import jax
import jax.numpy as jnp
import ml_dtypes
import numpy as np
from jax import lax
from jax.experimental import pallas as pl
from jax.experimental.pallas import tpu as pltpu
from jax.sharding import PartitionSpec as P

STENCIL = (
    -5369.0 / 1800.0,
    12.0 / 7.0,
    -15.0 / 56.0,
    10.0 / 189.0,
    -1.0 / 112.0,
    2.0 / 1925.0,
    -1.0 / 16632.0,
)
SPACING = 0.75
COEF = tuple(-0.5 / (SPACING * SPACING) * c for c in STENCIL)
W = 6
F32, BF16 = jnp.float32, jnp.bfloat16
VM = pl.BlockSpec(memory_space=pltpu.VMEM)
SM = pl.BlockSpec(memory_space=pltpu.SMEM)
ANY = pl.BlockSpec(memory_space=pl.ANY)
MIB = 1 << 20
GRID = ("chip", "core")


def in_hbm_type(array):
    return pltpu.HBM(array.shape, array.dtype)


def in_vmem(value):
    return pltpu.with_memory_space_constraint(value, pltpu.VMEM)


def in_hbm(value):
    return pltpu.with_memory_space_constraint(value, pltpu.HBM)


def circulant(n):
    m = np.zeros((n, n), np.float64)
    for k in range(1, W + 1):
        for i in range(n):
            m[i, (i + k) % n] += COEF[k]
            m[i, (i - k) % n] += COEF[k]
    high = m.astype(ml_dtypes.bfloat16)
    low = (m - high.astype(np.float64)).astype(ml_dtypes.bfloat16)
    return high, low


def plane_of(m, core):
    return m + core * (2 * W - 1 - 2 * m)


def core_index():
    return lax.axis_index("core")


def rows_of(t):
    return pl.ds(pl.multiple_of(t * 8, 8), 8)


def call(kernel, out_shape, in_specs, out_specs, scratch=(), limit=24):
    return pl.pallas_call(
        kernel,
        out_shape=out_shape,
        in_specs=in_specs,
        out_specs=out_specs,
        scratch_shapes=list(scratch),
        compiler_params=pltpu.CompilerParams(vmem_limit_bytes=limit * MIB),
    )


def source_kernel(orb, trial, ro, ri, a, b, sems):
    core = core_index()

    def copies(m):
        p = plane_of(m, core)
        return (
            pltpu.make_async_copy(orb.at[0, p], a.at[m], sems.at[0, m]),
            pltpu.make_async_copy(trial.at[p], b.at[m], sems.at[1, m]),
        )

    for m in range(2 * W):
        for c in copies(m):
            c.start()
    for m in range(2 * W):
        for c in copies(m):
            c.wait()
        out = ro if m < W else ri
        out[m % W] = a[m] * b[m]


def part_rows(d, me, count, part):
    quarter = lax.rem(me + d, count)
    return quarter * part


def local_kernel(fo, fi, hi_halo, pot, orb, energy, mz, my, *refs, stage, count):
    gi, po, tile, own_out, kept, *parts = refs[-count - 9 : -5]
    orb_v, own, yz, sems, more_sems = refs[-5:]
    parts = [own, *parts]
    core, me = core_index(), lax.axis_index("orb")
    nz = fo.shape[2]
    part = own.shape[1]
    first = 0 if stage == 1 else W
    loads = [pltpu.make_async_copy(orb.at[0, plane_of(first + m, core)], orb_v.at[m], sems.at[m]) for m in range(W)]
    stores = (
        pltpu.make_async_copy(fo, kept.at[pl.ds(0, W)], more_sems.at[0]),
        pltpu.make_async_copy(fi, kept.at[pl.ds(W, W)], more_sems.at[1]),
    )
    store_own = pltpu.make_async_copy(own, own_out, more_sems.at[2])
    for c in loads:
        c.start()

    for half, ref in enumerate((fo, fi)):

        def one(m, _, ref=ref, half=half):
            v = ref[m]
            high = v.astype(BF16)
            low = (v - high.astype(F32)).astype(BF16)
            dot = functools.partial(jnp.dot, preferred_element_type=F32)
            acc = dot(high, mz[0]) + dot(low, mz[0]) + dot(high, mz[1])
            acc = acc + (dot(my[0], high) + dot(my[1], high) + dot(my[0], low))
            yz[half * W + m] = acc
            return 0

        lax.fori_loop(0, W, one, 0)

    for c in loads:
        c.wait()
    for c in stores:
        c.start()
    diag = 3.0 * COEF[0] - energy[0]
    acc = jnp.zeros((8, 128), F32)
    for d in range(count):
        start = part_rows(d, me, count, part)

        def column(t, acc, d=d, start=start):
            rows = pl.ds(pl.multiple_of(start + t * 8, 8), 8)
            for h in range(nz // 128):
                lanes = slice(128 * h, 128 * h + 128)
                line = [fo[m, rows, lanes] for m in range(W)]
                line += [fi[m, rows, lanes] for m in range(W)]
                line += [hi_halo[W - 1 - m, rows, lanes] for m in range(W)]
                for m in range(2 * W):
                    if stage < 2:
                        acc = acc + line[m] * line[m]
                    out = (pot[plane_of(m, core), rows, lanes] + diag) * line[m]
                    out = out + yz[m, rows, lanes]
                    for k in range(1, W + 1):
                        pair = line[m + k] if m < k else line[m + k] + line[m - k]
                        out = out + COEF[k] * pair
                    if m < W:
                        po[m, rows, lanes] = out
                        if stage == 1:
                            parts[d][m, rows_of(t), lanes] = orb_v[m, rows, lanes] * line[m]
                    else:
                        gi[m - W, rows, lanes] = out
                        if stage != 1:
                            at = m if stage == 2 and d else m - W
                            parts[d][at, rows_of(t), lanes] = orb_v[m - W, rows, lanes] * out
            return acc

        acc = lax.fori_loop(0, part // 8, column, acc)
    tile[...] = acc
    store_own.start()
    for c in stores:
        c.wait()
    store_own.wait()


def with_halo(po, ho, rows, lanes):
    halo = [ho[j, rows, lanes] for j in range(W)]
    outs = []
    for m in range(W):
        out = po[m, rows, lanes]
        for k in range(m + 1, W + 1):
            out = out + COEF[k] * halo[k - m - 1]
        outs.append(out)
    return outs


def halo_kernel(po, ho, *refs):
    go = refs[-1]

    def column(t, _):
        rows = rows_of(t)
        for h in range(po.shape[2] // 128):
            lanes = slice(128 * h, 128 * h + 128)
            for m, out in enumerate(with_halo(po, ho, rows, lanes)):
                go[m, rows, lanes] = out
        return 0

    lax.fori_loop(0, po.shape[1] // 8, column, 0)


def whole_sum(tile):
    return jnp.sum(tile, keepdims=True)


def broad(scalar, shape=(8, 128)):
    return jnp.broadcast_to(scalar, shape)


def sums_kernel(r, t_kept, orb, uo, ui, vi, rr_tile, tt_tile, *refs):
    rows_out, inner, to, orb_o, r_v, ti, sems = refs[-7:]
    core = core_index()
    ro, ri = r_v.at[pl.ds(0, W)], r_v.at[pl.ds(W, W)]
    loads = (
        pltpu.make_async_copy(r, r_v, sems.at[0]),
        pltpu.make_async_copy(t_kept.at[pl.ds(W, W)], ti, sems.at[1]),
        pltpu.make_async_copy(t_kept.at[pl.ds(0, W)], to, sems.at[2]),
        *(pltpu.make_async_copy(orb.at[0, plane_of(m, core)], orb_o.at[m], sems.at[3 + m]) for m in range(W)),
    )
    for c in loads:
        c.start()
    loads[0].wait()
    steps = uo.shape[1] // 8
    zero = jnp.zeros((8, 128), F32)

    def cells(t):
        for h in range(uo.shape[2] // 128):
            for m in range(W):
                yield m, rows_of(t), slice(128 * h, 128 * h + 128)

    def cross(t, acc):
        for at in cells(t):
            acc = acc + ro[at] * uo[at] + ri[at] * ui[at]
        return acc

    rr = whole_sum(rr_tile[...])
    ru = whole_sum(lax.fori_loop(0, steps, cross, zero))
    theta = broad(jnp.where(rr > 0.0, ru / jnp.where(rr > 0.0, rr, 1.0), 0.0))

    def squares(t, accs):
        s0, s1, t0, t1 = accs
        for at in cells(t):
            for r, u in ((ro, uo), (ri, ui)):
                x = u[at] - theta * r[at]
                s0, s1 = s0 + x * x, s1 + x * r[at]
            x = vi[at] - theta * ti[at]
            t0, t1 = t0 + x * x, t1 + x * ti[at]
        return s0, s1, t0, t1

    loads[1].wait()
    s0, s1, t0, t1 = lax.fori_loop(0, steps, squares, (zero,) * 4)
    row = [rr, whole_sum(tt_tile[...]), whole_sum(s0), whole_sum(s1)]
    rows_out[...] = jnp.concatenate([broad(x, (1, 128)) for x in row] + [theta[:4]], axis=0)
    inner[0], inner[1] = t0, t1
    for c in loads[2:]:
        c.wait()


def last_kernel(po, ho, to, orb, rows_in, inner, *refs, count):
    tile, own_out, *outs, own, sem = refs[-count - 3 :]
    for done, out in zip(refs[: count - 1], outs):
        for m in range(W, 2 * W):
            out[m] = done[m]
    outs = [own, *outs]
    me = lax.axis_index("orb")
    theta = broad(rows_in[4:5])
    part = outs[0].shape[1]
    accs = inner[0], inner[1]
    for d in range(count):
        start = part_rows(d, me, count, part)

        def column(step, accs, d=d, start=start):
            t0, t1 = accs
            there = pl.ds(pl.multiple_of(start + step * 8, 8), 8)
            for h in range(po.shape[2] // 128):
                lanes = slice(128 * h, 128 * h + 128)
                for m, v in enumerate(with_halo(po, ho, there, lanes)):
                    t = to[m, there, lanes]
                    x = v - theta * t
                    t0, t1 = t0 + x * x, t1 + x * t
                    outs[d][m, rows_of(step), lanes] = orb[m, there, lanes] * v
            return t0, t1

        accs = lax.fori_loop(0, part // 8, column, accs)
        if d == 0:
            store_own = pltpu.make_async_copy(own, own_out, sem.at[0])
            store_own.start()
    lane = lax.broadcasted_iota(jnp.int32, (8, 128), 1)
    row = jnp.zeros((8, 128), F32)
    for i in range(5):
        row = jnp.where(lane == i, broad(rows_in[i : i + 1]), row)
    for i, x in enumerate(accs):
        row = jnp.where(lane == 5 + i, broad(whole_sum(x)), row)
    tile[...] = row
    store_own.wait()


def copies_kernel(row, other, out):
    mine = lax.broadcasted_iota(jnp.int32, row.shape, 0) == core_index()
    both = jnp.where(mine, row[...], other[...])
    for i in range(out.shape[0]):
        out[i] = both


def coefficient_kernel(shares, freq, out):
    w2 = freq[0] * freq[0]
    share = jnp.concatenate([shares[:, 0, :], shares[:, 1, :]], axis=0)
    rr, tt, s0, s1, own, t0, t1 = (share[:, i : i + 1] for i in range(7))

    def total(x):
        return jnp.sum(x, axis=0, keepdims=True)

    rr0, tt0 = total(rr), total(tt)
    theta = tt0 / rr0
    off = jnp.broadcast_to(theta, own.shape) - own
    alpha = 1.0 / (theta + w2)
    rr1 = alpha * alpha * total(s0 - 2.0 * off * s1 + off * off * rr)
    tt1 = alpha * alpha * total(t0 - 2.0 * off * t1 + off * off * tt)
    ratio = rr1 / rr0
    beta = rr1 / (tt1 + w2 * rr1 - ratio * rr1 / alpha)
    p = alpha + beta * ratio + beta * alpha * theta
    q = -beta * alpha
    both = jnp.concatenate([broad(p, (4, 128)), broad(q, (4, 128))], axis=0)
    for i in range(out.shape[0]):
        out[i] = both


def both_of(coefs, n, shape):
    one = coefs[n]
    return tuple(broad(one[4 * i : 4 * i + 1, 0:1], shape) for i in range(2))


def solution_kernel(r, u, coefs, sol, rbuf, ubuf, xbuf, in_sems, out_sems):
    core = core_index()

    def fields(m):
        return (
            pltpu.make_async_copy(r.at[m], rbuf.at[m], in_sems.at[0, m]),
            pltpu.make_async_copy(u.at[m], ubuf.at[m], in_sems.at[1, m]),
        )

    def store(m):
        return pltpu.make_async_copy(xbuf.at[m], sol.at[0, plane_of(m, core)], out_sems.at[m])

    for m in range(2 * W):
        for c in fields(m):
            c.start()
    p, q = both_of(coefs, 0, (8, r.shape[2]))
    for m in range(2 * W):
        for c in fields(m):
            c.wait()

        def row(t, _, m=m):
            rows = rows_of(t)
            xbuf[m, rows, :] = p * rbuf[m, rows, :] + q * ubuf[m, rows, :]
            return 0

        lax.fori_loop(0, r.shape[1] // 8, row, 0, unroll=8)
        store(m).start()
    for m in range(2 * W):
        store(m).wait()


def density_kernel(coefs, *refs, count):
    ti, to, own_v, parts = refs[:count], refs[count : 2 * count], refs[2 * count : 2 * count + 2], refs[2 * count + 2 : -6]
    dens, t_all, own, dbuf, load_sems, sems = refs[-6:]
    parts = [own, *parts]
    core, me = core_index(), lax.axis_index("orb")
    loads = [[], []]
    for half, sources in enumerate((to, ti)):
        places = pl.ds(half * W, W)
        pairs = [(x, t_all.at[d, places]) for d, x in enumerate(sources)] + [(own_v[half], own.at[places])]
        loads[half] = [pltpu.make_async_copy(x, y, load_sems.at[half, i]) for i, (x, y) in enumerate(pairs)]
    for c in loads[0] + loads[1]:
        c.start()
    pq = [both_of(coefs, lax.rem(me - d + count, count), (8, own.shape[2])) for d in range(count)]
    pq = [(-4.0 * p, -4.0 * q) for p, q in pq]

    def store(m):
        return pltpu.make_async_copy(dbuf.at[m], dens.at[plane_of(m, core)], sems.at[m])

    for m in range(2 * W):
        if m % W == 0:
            for c in loads[m // W]:
                c.wait()

        def part(t, _, m=m):
            rows = rows_of(t)
            acc = None
            for d in range(count):
                term = pq[d][0] * t_all[d, m, rows, :] + pq[d][1] * parts[d][m, rows, :]
                acc = term if acc is None else acc + term
            dbuf[m, rows, :] = acc
            return 0

        lax.fori_loop(0, dbuf.shape[1] // 8, part, 0, unroll=2)
        store(m).start()
    for m in range(2 * W):
        store(m).wait()


def shift(value, axis, count, d):
    return lax.ppermute(value, axis, [(i, (i + d) % count) for i in range(count)])


def body(orbitals, potential, trial_potential, eigenvalues, frequency, *, norb, ngrid):
    _, nx, ny, nz = orbitals.shape
    half = pltpu.VMEM((W, ny, nz), F32)
    tile = jax.ShapeDtypeStruct((8, 128), F32)
    part = ny // norb
    whole = jax.ShapeDtypeStruct((2 * W, ny, nz), F32)
    piece = pltpu.VMEM((W, part, nz), F32)
    long_piece = pltpu.VMEM((2 * W, part, nz), F32)
    mz = jnp.asarray(np.stack(circulant(nz)))
    my = jnp.asarray(np.stack(circulant(ny)))
    orbitals, trial_potential = in_hbm(orbitals), in_hbm(trial_potential)

    inner_pairs = [(i, i ^ 1) for i in range(ngrid)]
    outer_pairs = [(i, i + 1) for i in range(1, ngrid - 1, 2)]
    outer_pairs += [(j, i) for i, j in outer_pairs]

    def outer_swap(x):
        with jax.named_scope("outer_swap"):
            return in_vmem(lax.ppermute(x, GRID, outer_pairs))

    def inner_swap(x):
        with jax.named_scope("inner_swap"):
            return in_vmem(lax.ppermute(x, GRID, inner_pairs))

    def local(stage, fo, fi, hi, *after):
        parts_type = long_piece if stage == 2 else piece
        gi, po, out, own, kept, *parts = call(
            functools.partial(local_kernel, stage=stage, count=norb),
            (half, half, tile, in_hbm_type(piece), in_hbm_type(whole)) + (parts_type,) * (norb - 1),
            [VM] * 4 + [ANY, SM, VM, VM] + [ANY] * len(after),
            (VM, VM, VM, ANY, ANY) + (VM,) * (norb - 1),
            [
                pltpu.VMEM(half.shape, F32),
                pltpu.VMEM(piece.shape, F32),
                pltpu.VMEM(whole.shape, F32),
                pltpu.SemaphoreType.DMA((W,)),
                pltpu.SemaphoreType.DMA((3,)),
            ],
            limit=12,
        )(fo, fi, hi, potential, orbitals, eigenvalues, mz, my, *after)
        return gi, po, out, kept, [own, *parts]

    def add_halo(po, ho, *after):
        return call(halo_kernel, half, [VM, VM] + [VM] * len(after), VM, limit=4)(po, ho, *after)

    def send_parts(parts):
        with jax.named_scope("density_parts"):
            return [parts[0]] + [shift(parts[d], "orb", norb, d) for d in range(1, norb)]

    ro, ri = call(
        source_kernel,
        (half, half),
        [ANY, ANY],
        (VM, VM),
        [pltpu.VMEM(whole.shape, F32), pltpu.VMEM(whole.shape, F32), pltpu.SemaphoreType.DMA((2, 2 * W))],
        limit=10,
    )(orbitals, trial_potential)
    ho = outer_swap(ro)
    ti, po, rr, r_kept, parts = local(0, ro, ri, inner_swap(ri))
    parts_ti = send_parts(parts)
    to = add_halo(po, ho)

    ho = outer_swap(to)
    ui, po, tt, t_kept, parts = local(1, to, ti, inner_swap(ti))
    parts_to = send_parts(parts)
    uo = add_halo(po, ho, *parts_ti[1:])

    ho = outer_swap(uo)
    vi, po, _, u_kept, parts = local(2, uo, ui, inner_swap(ui))
    shares, inner, to, orb_o = call(
        sums_kernel,
        (tile, jax.ShapeDtypeStruct((2, 8, 128), F32), half, half),
        [ANY] * 3 + [VM] * 5,
        (VM,) * 4,
        [pltpu.VMEM(whole.shape, F32), pltpu.VMEM(half.shape, F32), pltpu.SemaphoreType.DMA((3 + W,))],
        limit=5,
    )(r_kept, t_kept, orbitals, uo, ui, vi, rr, tt)

    shares, own_vo, *parts_v = call(
        functools.partial(last_kernel, count=norb),
        (tile, in_hbm_type(piece)) + (long_piece,) * (norb - 1),
        [VM] * (4 + 2 * norb),
        (VM, ANY) + (VM,) * (norb - 1),
        [pltpu.VMEM(piece.shape, F32), pltpu.SemaphoreType.DMA((1,))],
        limit=8,
    )(po, ho, to, orb_o, shares, inner, *parts[1:], *parts_to[1:])
    with jax.named_scope("density_parts"):
        parts_v = [in_vmem(shift(x, "orb", norb, d)) for d, x in enumerate(parts_v, 1)]
    with jax.named_scope("all_shares"):
        shares = call(
            copies_kernel, jax.ShapeDtypeStruct((ngrid // 2, 8, 128), F32), [VM, VM], VM, limit=4
        )(shares, lax.ppermute(shares, GRID, inner_pairs))
        shares = lax.all_to_all(shares, "chip", 0, 0, tiled=True)
    coefs = call(coefficient_kernel, jax.ShapeDtypeStruct((norb, 8, 128), F32), [VM, SM], VM, limit=4)(
        shares, frequency
    )
    with jax.named_scope("all_coefficients"):
        all_coefs = lax.all_to_all(coefs, "orb", 0, 0, tiled=True)
    solution = call(
        solution_kernel,
        in_hbm_type(jax.ShapeDtypeStruct((1, nx, ny, nz), F32)),
        [ANY, ANY, VM],
        ANY,
        [pltpu.VMEM(whole.shape, F32)] * 3 + [pltpu.SemaphoreType.DMA((2, nx)), pltpu.SemaphoreType.DMA((nx,))],
        limit=9,
    )(in_hbm(r_kept), in_hbm(u_kept), coefs)
    waiting = [in_hbm(x) for x in (*parts_ti, *parts_to, own_vo, parts[0])]
    density = call(
        functools.partial(density_kernel, count=norb),
        in_hbm_type(long_piece),
        [VM] + [ANY] * len(waiting) + [VM] * (norb - 1),
        ANY,
        [
            pltpu.VMEM((norb, *long_piece.shape), F32),
            pltpu.VMEM(long_piece.shape, F32),
            pltpu.VMEM(long_piece.shape, F32),
            pltpu.SemaphoreType.DMA((2, norb + 1)),
            pltpu.SemaphoreType.DMA((nx,)),
        ],
        limit=8,
    )(all_coefs, *waiting, *parts_v)
    return solution, density


def solution(mesh):
    norb, ngrid = mesh.shape["orb"], mesh.shape["grid"]
    mesh = jax.sharding.Mesh(mesh.devices.reshape(norb, ngrid // 2, 2), ("orb", *GRID))
    in_specs = (
        P("orb", GRID, None, None),
        P(GRID, None, None),
        P(GRID, None, None),
        P("orb"),
        P(),
    )
    out_specs = (P("orb", GRID, None, None), P(GRID, "orb", None))
    step = functools.partial(body, norb=norb, ngrid=ngrid)
    return jax.shard_map(step, mesh=mesh, in_specs=in_specs, out_specs=out_specs, check_vma=False)
```
